1024 devices in a mesh: ctx: 16 (over x_lo, y), exp: 64 (over x_hi, z, core).
Axes of the slice: x: 8 (x_hi: 4, x_lo: 2; x = x_hi * 2 + x_lo), y: 8, z: 8, core: 2. Of those that a mesh axis runs over, the one named last changes fastest.
Arguments:
- queries: bfloat16 [2048, 36864], P('ctx', 'exp'), may hold values from -400 to 400
- latents: bfloat16 [2048, 576], P('ctx'), may hold values from -6 to 6
- group_order: int32 [64], replicated, may hold values from 0 to 63, each once
- hidden_b: bfloat16 [512, 7168], P('exp', 'ctx'), may hold values from -6 to 6
- expert_ids: int32 [512, 8], P('exp'), may hold values from 0 to 63, all different within a row; in each aligned block of 8 rows (0 to 7, 8 to 15, ...) at most 2 rows name the same one
- gate_fixed: int32 [512, 8], P('exp'), may hold values from 4096 to 32767
- w_gate: bfloat16 [64, 7168, 1024], P('exp', 'ctx'), may hold values from -0.0625 to 0.0625
- w_up: bfloat16 [64, 7168, 1024], P('exp', 'ctx'), may hold values from -0.0625 to 0.0625
- w_down: bfloat16 [64, 1024, 7168], P('exp', None, 'ctx'), may hold values from -0.1875 to 0.1875
Outputs:
- attn_out: bfloat16 [2048, 32768], P('ctx', 'exp')
- moe_out: bfloat16 [512, 7168], P('exp', 'ctx')
The draws below stay inside these ranges and needn't reach their ends.
Inputs may be any that keep to these rules, and one draw needn't show every extreme that they name: `group_order`: each block position appears once. `expert_ids`: each row names 8 different experts. Within the 8 rows of one index of exp (aligned blocks of 8 rows) no expert is named more than 2 times, a bound that some block reaches.
All inputs are finite; a program needn't handle non-finite values.
Results may differ from the reference program's by a relative error of at most 0.006.
Values may be sent and summed in bfloat16 or wider, within the bound.
A program may use at most 32 MiB of HBM per device.

```python
import math
import jax
import jax.numpy as jnp
import numpy as np
from jax import lax

D = 7168
KV_RANK = 512
KVW = 576
TOPK = 8
HEADS = 64
EXP_FF = 1024
EXPERTS = 64
SUB = 4
LEN_DEV = 128
LENGTH = 2048
BLOCKS = 64
TOK_DEV = 8
TOKENS = 512
CAP = 2
N_EXP = 64


def latent_table(key, pair_mix):
    block_len = LEN_DEV // SUB
    base = jnp.clip(jax.random.normal(key, (LENGTH, KVW), jnp.float32), -6.0, 6.0)
    row_ids = jnp.arange(LENGTH)[:, None]
    col_ids = jnp.arange(KVW)[None, :]
    pick = ((row_ids % block_len == 1) & (col_ids >= KV_RANK)).astype(jnp.float32) * pair_mix
    return base * (1.0 - pick)


def draw_latents(key, part):
    table = latent_table(key, 0.0)
    return table.astype(jnp.bfloat16)


def draw_queries(key, part):
    key = jax.random.fold_in(key, 2)
    values = jnp.clip(0.6 * jax.random.normal(key, (LENGTH, HEADS, KVW), jnp.float32), -4.0, 4.0)
    return values.reshape(LENGTH, HEADS * KVW).astype(jnp.bfloat16)


def place_ends(array, key, least, largest):
    longest = array.shape.index(max(array.shape))
    spots = []
    for shift in (0, 1):
        where = [jax.random.randint(jax.random.fold_in(key, axis), (), 0, length) for axis, length in enumerate(array.shape)]
        where[longest] = (where[longest] + shift) % array.shape[longest]
        spots.append(tuple(where))
    return array.at[spots[0]].set(least).at[spots[1]].set(largest)


def steps_of(key, dims, pieces, smallest, high):
    def one(axis_at, shards_of):
        draws = jax.random.uniform(jax.random.fold_in(jax.random.fold_in(key, 6), axis_at), (shards_of,), jnp.float32, smallest / len(pieces), high / len(pieces))
        return jnp.repeat(jnp.exp(draws), dims[axis_at] // shards_of).reshape((-1,) + (1,) * (len(dims) - axis_at - 1))

    level = one(*pieces[0])
    for cut in pieces[1:]:
        level = level * one(*cut)
    return level


def shared_out(stream_key, own, number, rows, number_of, top, limit, slope):
    order = jax.random.permutation(stream_key, number_of)
    crowded, common = load_shares(number_of, rows * top, limit, slope, True), load_shares(number_of, rows * top, limit, slope, False)
    places = jnp.arange(number_of)

    def named(sizes, rotation):
        used = int((sizes > 0).sum())
        fixed = max(1, used // 4)
        moved = fixed + (places - fixed + rotation * (used - fixed)) % max(1, number_of - fixed)
        return jnp.zeros((number_of,), jnp.int32).at[order[jnp.where(places < fixed, places, moved)]].set(jnp.asarray(sizes, jnp.int32))

    sizes = jnp.where(number % 4 == 0, named(crowded, number // 4), named(common, number - number // 4 - 1))
    mixed = jax.random.permutation(jax.random.fold_in(own, 3), number_of)
    giver, receiver = mixed[0:number_of // 2 * 2:2], mixed[1:number_of // 2 * 2:2]
    slack = jnp.minimum(sizes[giver] - 1, limit - sizes[receiver]) // 2
    slack = jnp.where((giver == order[0]) | (receiver == order[0]) | (sizes[receiver] == 0), 0, jnp.maximum(slack, 0))
    moved = jax.random.randint(jax.random.fold_in(own, 4), (number_of // 2,), 0, 1 << 20) % (slack + 1)
    sizes = sizes.at[giver].add(-moved).at[receiver].add(moved)
    items = jnp.searchsorted(jnp.cumsum(sizes), jnp.arange(rows * top), side="right").astype(jnp.int32)
    listing = items.reshape(top, rows).T
    listing = listing[jax.random.permutation(jax.random.fold_in(own, 1), rows)]
    rotation = jax.random.randint(jax.random.fold_in(own, 2), (rows, 1), 0, top)
    return jnp.take_along_axis(listing, (jnp.arange(top)[None, :] + rotation) % top, axis=1)


def load_shares(count, total, limit, slope, full):
    portions = [(1 << 20) // math.isqrt(rank ** slope) + 1 for rank in range(1, count + 1)]
    largest = limit if full else min(limit, max(-(-total // count), total * portions[0] // sum(portions)))
    least = 1 if total - largest >= count - 1 else 0
    given, rest = [largest] + [least] * (count - 1), total - largest - least * (count - 1)
    while rest > 0:
        candidates = [i for i in range(1, count) if given[i] < largest] or [i for i in range(1, count) if given[i] < limit]
        mass, left = sum([portions[i] for i in candidates]), rest
        for i in candidates:
            more = min(limit - given[i], max(1, left * portions[i] // mass), rest)
            given[i] = given[i] + more
            rest = rest - more
    return np.array(given)


def scatter_about(key, extent, width, most, split=(), kind=jnp.bfloat16):
    entries = jax.random.normal(key, extent, jnp.float32) * width
    if len(split) > 0:
        entries = steps_of(key, extent, split, -0.22, 0.18) * entries
    return jnp.clip(entries, min=-most, max=most).astype(kind)


def setup_inputs(seed: int = 0) -> dict:
    arg_keys = jax.random.split(jax.random.key(seed), 10)
    queries = draw_queries(jax.random.fold_in(arg_keys[9], 71), 0)
    latents = draw_latents(jax.random.fold_in(arg_keys[9], 71), 0)
    group_order = jax.random.permutation(arg_keys[2], BLOCKS).astype(jnp.int32)
    hidden_b = scatter_about(arg_keys[3], (TOKENS, D), 1.0, 6.0, ((0, 64), (1, 16)))
    expert_ids_keys = jax.random.split(jax.random.fold_in(arg_keys[4], 1), TOKENS // TOK_DEV)
    expert_ids_turns = jax.random.permutation(jax.random.fold_in(arg_keys[4], 3), TOKENS // TOK_DEV)
    expert_ids = jax.vmap(lambda own, number: shared_out(jax.random.fold_in(arg_keys[4], 2), own, number, TOK_DEV, EXPERTS, TOPK, CAP, 2))(expert_ids_keys, expert_ids_turns).reshape((TOKENS, TOPK))
    gate_fixed = place_ends(jax.random.randint(arg_keys[5], (TOKENS, TOPK), 4096, 32768), jax.random.fold_in(arg_keys[5], 1), 4096, 32767).astype(jnp.int32)
    w_gate = scatter_about(arg_keys[6], (EXPERTS, D, EXP_FF), D ** -0.5, 0.0625, ((0, 64), (1, 16)))
    w_up = scatter_about(arg_keys[7], (EXPERTS, D, EXP_FF), D ** -0.5, 0.0625, ((0, 64), (1, 16)))
    w_down = scatter_about(arg_keys[8], (EXPERTS, EXP_FF, D), EXP_FF ** -0.5, 0.1875, ((0, 64), (2, 16)))
    return {"queries": queries, "latents": latents, "group_order": group_order, "hidden_b": hidden_b, "expert_ids": expert_ids, "gate_fixed": gate_fixed, "w_gate": w_gate, "w_up": w_up, "w_down": w_down}


SCALE = 1.0 / math.sqrt(192.0)

def prompt_positions(group_order, row_index, block_rows):
    owner = row_index // block_rows
    group_ids = jnp.arange(group_order.shape[0], dtype=jnp.int32)
    matches = (owner[:, None] == group_ids[None, :]).astype(jnp.int32)
    return lax.optimization_barrier(jnp.sum(matches * group_order[None, :], axis=1)) * block_rows + row_index % block_rows

def attend_head(q_head, keys, query_pos, key_pos):
    scores = lax.dot_general(q_head, keys, (((1,), (1,)), ((), ())), preferred_element_type=jnp.float32) * SCALE
    scores = jnp.where(key_pos[None, :] <= query_pos[:, None], scores, jnp.float32(-1e+30))
    top_score = lax.optimization_barrier(jnp.max(scores, axis=1, keepdims=True))
    raised = jnp.exp(scores - top_score)
    probs = (raised / lax.optimization_barrier(jnp.sum(raised, axis=1, keepdims=True))).astype(jnp.bfloat16)
    return jnp.dot(probs, keys[:, :KV_RANK], preferred_element_type=jnp.float32).astype(jnp.bfloat16)

def reference(queries, latents, group_order, hidden_b, expert_ids, gate_fixed, w_gate, w_up, w_down):
    row_index = jnp.arange(LENGTH, dtype=jnp.int32)
    positions = prompt_positions(group_order, row_index, LEN_DEV // SUB)
    per_head = jnp.swapaxes(queries.reshape(LENGTH, HEADS, KVW), 0, 1)
    outputs = lax.map(lambda q_head: attend_head(q_head, latents, positions, positions), per_head)
    attn_out = jnp.swapaxes(outputs, 0, 1).reshape(LENGTH, HEADS * KV_RANK)
    gates = gate_fixed.astype(jnp.float32) / 32768.0
    slots_all = N_EXP * CAP

    def one_expert(total, packed):
        gate_w, up_w, down_w, expert_index = packed
        hit = expert_ids == expert_index
        coef = lax.optimization_barrier(jnp.sum(jnp.where(hit, gates, jnp.float32(0.0)), axis=1))
        used = jnp.any(hit, axis=1)
        picked = jnp.nonzero(used, size=slots_all, fill_value=0)[0].astype(jnp.int32)
        valid = jnp.arange(slots_all, dtype=jnp.int32) < jnp.sum(used.astype(jnp.int32))
        chosen = hidden_b[picked]
        pre_gate = jnp.dot(chosen, gate_w, preferred_element_type=jnp.float32)
        pre_up = jnp.dot(chosen, up_w, preferred_element_type=jnp.float32)
        inner = (jax.nn.silu(pre_gate) * pre_up).astype(jnp.bfloat16)
        expert_out = jnp.dot(inner, down_w, preferred_element_type=jnp.float32).astype(jnp.bfloat16)
        weight = jnp.where(valid, coef[picked], jnp.float32(0.0))
        total = total.at[picked].add(weight[:, None] * expert_out.astype(jnp.float32))
        return (total, None)
    start_total = jnp.zeros((TOKENS, D), jnp.float32)
    total, _ = lax.scan(one_expert, start_total, (w_gate, w_up, w_down, jnp.arange(EXPERTS, dtype=jnp.int32)))
    return (attn_out, total.astype(jnp.bfloat16))
```

```python
import functools
import math

import jax
import jax.numpy as jnp
from jax import lax
from jax.experimental import pallas as pl
from jax.experimental.pallas import tpu as pltpu
from jax.sharding import PartitionSpec as P

MESH = pl.DeviceIdType.MESH
SCALE = 1.0 / math.sqrt(192.0)
KV_RANK = 512
BF = jnp.bfloat16
F32 = jnp.float32
I32 = jnp.int32


def iota(shape, dim):
    return lax.broadcasted_iota(I32, shape, dim)


def dot(a, b, dims=((1,), (0,))):
    return lax.dot_general(a, b, (dims, ((), ())), preferred_element_type=F32)


def kernel(
    q_hbm, lat_hbm, go_ref, hid_ref, ids_ref, gate_ref, wg_hbm, wu_hbm, wd_hbm,
    attn_ref, moe_ref,
    q, lat, wg, wu, wd, pay, hall, part, xin, yin, inner, zbuf, ret, back, comb_hi, comb_lo, scores,
    wsem, qsem, lsem, hx_s, hx_r, hz_s, hz_r, hc_s, hc_r,
    rx_s, rx_r, ry_s, ry_r, ay_s, ay_r, ax_s, ax_r, rt_s, rt_r,
    ly_s, ly_r, lx_s, lx_r, lc_s, lc_r,
):
    c = lax.axis_index("ctx")
    e = lax.axis_index("exp")
    xl, y = c // 8, c % 8
    xh, z, core = e // 16, (e // 2) % 8, e % 2

    def dev(c_, e_):
        return {"ctx": c_, "exp": e_}

    def exp_at(xh_, z_, core_):
        return (xh_ * 8 + z_) * 2 + core_

    def x_peer(k):
        return dev(c, exp_at((xh + k) % 4, z, core))

    def z_peer(k):
        return dev(c, exp_at(xh, (z + k) % 8, core))

    def y_peer(k):
        return dev(xl * 8 + (y + k) % 8, e)

    sibling = dev(c, exp_at(xh, z, 1 - core))
    pair = dev((c + 8) % 16, e)
    far_pair = dev((c + 8) % 16, exp_at((xh + 3 + 2 * xl) % 4, z, core))

    def send(src, dst, ss, rs, to):
        pltpu.make_async_remote_copy(
            src_ref=src, dst_ref=dst, send_sem=ss, recv_sem=rs, device_id=to, device_id_type=MESH
        ).start()

    def wait(like, sem):
        pltpu.make_async_copy(like, like, sem).wait()

    barrier = pltpu.get_barrier_semaphore()

    def hello(to):
        pl.semaphore_signal(barrier, inc=1, device_id=to, device_id_type=MESH)

    @pl.loop(1, 8)
    def _(k):
        hello(z_peer(k))

    @pl.loop(1, 4)
    def _(k):
        hello(x_peer(k))

    @pl.loop(1, 8)
    def _(k):
        hello(y_peer(k))

    hello(sibling)
    hello(pair)
    hello(far_pair)

    half = pl.ds(pl.multiple_of(core * 64, 64), 64)
    lat_copy = pltpu.make_async_copy(lat_hbm.at[half], lat.at[c, half], lsem)
    lat_copy.start()
    w_copies = [
        pltpu.make_async_copy(wg_hbm.at[0], wg.at[pl.ds(0, 448)], wsem.at[0]),
        pltpu.make_async_copy(wu_hbm.at[0], wu.at[pl.ds(0, 448)], wsem.at[1]),
        pltpu.make_async_copy(wd_hbm.at[0], wd, wsem.at[2]),
    ]
    for cp in w_copies:
        cp.start()
    q_copy = pltpu.make_async_copy(q_hbm, q, qsem)
    q_copy.start()

    ids = ids_ref[...].astype(F32)
    pay[...] = jnp.zeros((8, 512), F32)
    pay[:, :448] = hid_ref[...].astype(F32)
    spread = (iota((8, 128), 1) == iota((8, 128), 0) + 64).astype(BF)
    pay[:, 384:] = pay[:, 384:] + dot(ids.astype(BF), spread)
    hall[core, z, xh] = jnp.concatenate([pay[:, :256], pay[:, 256:]], axis=0).astype(BF)
    for w in (wg, wu):
        w[448:, :] = jnp.zeros((64, 1024), BF)
    zbuf[:, 384:] = jnp.zeros((128, 128), F32)

    lat_copy.wait()
    pl.semaphore_wait(barrier, 20)

    @pl.loop(1, 4)
    def _(k):
        mine = hall.at[core, z, xh]
        send(mine, mine, hx_s, hx_r, x_peer(k))

    @pl.loop(1, 8)
    def _(k):
        mine = lat.at[c, half]
        send(mine, mine, ly_s, ly_r, y_peer(k))

    wait(hall.at[0, 0, pl.ds(0, 3)], hx_r)

    @pl.loop(1, 8)
    def _(k):
        mine = hall.at[core, z]
        send(mine, mine, hz_s, hz_r.at[k], z_peer(k))

    send(hall.at[core, z], hall.at[core, z], hc_s, hc_r, sibling)

    @pl.loop(0, 7)
    def _(n):
        k = (n // 2 + 1) * (1 - 2 * (n % 2)) + 8 * (n % 2)
        from_z = hall.at[core, (z + 8 - k) % 8]
        wait(from_z, hz_r.at[k])
        send(from_z, from_z, hc_s, hc_r, sibling)

    wait(hall.at[1 - core], hc_r)

    rows2d = hall[...].reshape(1024, 256)
    id_lane = iota((1024, 128), 1)
    named = jnp.where(
        (rows2d[:, 128:].astype(F32) == e.astype(F32)) & (id_lane >= 64) & (id_lane < 72), 1.0, 0.0
    ).astype(BF)
    hit = dot(jnp.ones((8, 128), BF), named, ((1,), (1,)))
    col = iota((8, 1024), 1)
    tok = col % 8
    hit = jnp.where((col // 8) % 2 == 1, hit, 0.0)
    upto = hit
    for step in (1, 2, 4):
        upto = upto + jnp.where(tok >= step, pltpu.roll(upto, step, 1), 0.0)
    code = jnp.where(hit > 0.5, (col // 16).astype(F32) * 2.0 + upto - hit, -1.0)
    row_id = iota((128, 1024), 0).astype(F32)
    pick_hi = jnp.where(code[:1] == row_id, 1.0, 0.0).astype(BF)
    pick_lo = jnp.where(pltpu.roll(code, 1024 - 8, 1)[:1] == row_id, 1.0, 0.0).astype(BF)
    x_lo = dot(pick_lo, rows2d).astype(BF)
    x_hi = dot(pick_hi, rows2d).astype(BF)

    w_copies[0].wait()
    w_copies[1].wait()
    gate_part = dot(x_lo, wg[:256, :]) + dot(x_hi, wg[256:, :])
    up_part = dot(x_lo, wu[:256, :]) + dot(x_hi, wu[256:, :])
    part[...] = jnp.concatenate(
        [gate_part.reshape(16, 8, 1024), up_part.reshape(16, 8, 1024)], axis=1
    ).astype(BF)

    def far_first(n):
        return 4 + (1 - 2 * (n % 2)) * ((n + 1) // 2)

    other = (1 - xl) * 8

    @pl.loop(0, 8)
    def _(n):
        send(part.at[other + (y + far_first(n)) % 8], xin.at[n], rx_s, rx_r.at[n], pair)

    own_half = lat.at[pl.ds(xl * 8, 8), half]
    wait(lat.at[pl.ds(0, 7), pl.ds(0, 64)], ly_r)
    send(own_half, own_half, lx_s, lx_r, far_pair)
    send(own_half, own_half, lc_s.at[0], lc_r.at[0], sibling)

    def add_pair(n):
        own = xl * 8 + (y + far_first(n)) % 8
        wait(xin.at[n], rx_r.at[n])
        return own, (part[own].astype(F32) + xin[n].astype(F32)).astype(BF)

    @pl.loop(0, 7)
    def _(n):
        own, total = add_pair(n)
        part[own] = total
        send(part.at[own], yin.at[y], ry_s, ry_r, y_peer(far_first(n)))

    _, own_total = add_pair(7)
    yin[y] = own_total
    wait(yin.at[pl.ds(0, 7)], ry_r)
    summed = jnp.sum(yin[...].astype(F32), axis=0)
    gate_sum, up_sum = summed[:8], summed[8:]
    act = gate_sum / (1.0 + jnp.exp(-gate_sum)) * up_sum
    inner[c] = jnp.concatenate([act[:, :512], act[:, 512:]], axis=0).astype(BF)

    @pl.loop(0, 7)
    def _(n):
        k = far_first(n)
        send(inner.at[c], inner.at[c], ay_s, ay_r.at[k], y_peer(k))

    send(inner.at[c], inner.at[c], ax_s, ax_r, pair)

    @pl.loop(0, 7)
    def _(n):
        k = (n // 2 + 1) * (1 - 2 * (n % 2)) + 8 * (n % 2)
        got = inner.at[xl * 8 + (y + 8 - k) % 8]
        wait(got, ay_r.at[k])
        send(got, got, ax_s, ax_r, pair)

    wait(inner.at[pl.ds(0, 8)], ax_r)
    acts = inner[...].astype(F32)
    w_copies[2].wait()
    zbuf[:, :448] = dot(acts[:, :8].reshape(128, 512).astype(BF), wd[:512, :]) + dot(
        acts[:, 8:].reshape(128, 512).astype(BF), wd[512:, :]
    )
    out_row = iota((512, 128), 0)
    in_row = iota((512, 128), 1)
    packed = jnp.zeros((512, 128), F32)
    for j in range(4):
        place = jnp.where(out_row == 4 * in_row + j, 1.0, 0.0).astype(BF)
        packed = packed + dot(place, zbuf[:, 128 * j : 128 * (j + 1)].astype(BF))
    ret[...] = packed.reshape(64, 8, 128).astype(BF)

    me = (core * 8 + z) * 4 + xh

    @pl.loop(1, 64)
    def _(k):
        g = (me + k) % 64
        to = dev(c, exp_at(g % 4, (g // 4) % 8, g // 32))
        send(ret.at[g], back.at[me], rt_s, rt_r, to)

    back[me] = ret[me]

    wait(own_half, lx_r)
    other_half = lat.at[pl.ds(other, 8), half]
    send(other_half, other_half, lc_s.at[1], lc_r.at[1], sibling)

    r_id = iota((512, 32), 0)
    q_id = iota((512, 32), 1)
    grp = r_id // 8
    expert_of_row = (((grp % 4) * 8 + (grp // 4) % 8) * 2 + grp // 32).astype(F32)
    diag = iota((8, 32), 0) == iota((8, 32), 1) % 8
    gates = gate_ref[...].astype(F32)
    found = jnp.zeros((512, 32), F32)
    gated = jnp.zeros((512, 32), F32)
    for k in range(8):
        id_row = jnp.sum(jnp.where(diag, ids[:, k : k + 1], 0.0), axis=0, keepdims=True)
        gate_row = jnp.sum(jnp.where(diag, gates[:, k : k + 1], 0.0), axis=0, keepdims=True)
        same = expert_of_row == id_row
        found = found + jnp.where(same, 1.0, 0.0)
        gated = gated + jnp.where(same, gate_row, 0.0)
    a_id, b_id = iota((32, 32), 0), iota((32, 32), 1)
    earlier = jnp.where((a_id // 8 == b_id // 8) & (a_id < b_id), 1.0, 0.0).astype(BF)
    before = dot(found.astype(BF), earlier)
    mine = (
        (found > 0.5) & (before == ((r_id // 4) % 2).astype(F32)) & (r_id % 4 == q_id // 8)
    )
    weight = jnp.where(mine, gated * (1.0 / 32768.0), 0.0)
    weight_hi = weight.astype(BF)
    comb_hi[...] = weight_hi
    comb_lo[...] = (weight - weight_hi.astype(F32)).astype(BF)

    go = go_ref[...].astype(F32)
    blk = iota((128, 64), 1)
    own_blk = c * 4 + iota((128, 64), 0) // 32
    query_pos = jnp.sum(jnp.where(blk == own_blk, go, 0.0), axis=1, keepdims=True) * 32.0 + (
        iota((128, 1), 0) % 32
    ).astype(F32)
    wait(own_half, lc_r.at[0])
    wait(own_half, lc_r.at[1])
    q_copy.wait()
    queries = q[...]

    def score(i, top):
        keys = lat[pl.ds(i * 2, 2)].reshape(256, 576)
        lane = iota((64, 256), 1)
        owner = jnp.where(iota((64, 256), 0) == i * 8 + lane // 32, 1.0, 0.0).astype(BF)
        base = dot(go.astype(BF), owner)
        key_pos = base * 32.0 + (iota((1, 256), 1) % 32).astype(F32)
        s = dot(queries, keys, ((1,), (1,))) * SCALE
        s = jnp.where(key_pos <= query_pos, s, -1e30)
        scores[i] = s
        return jnp.maximum(top, jnp.max(s, axis=1, keepdims=True))

    top = lax.fori_loop(0, 8, score, jnp.full((128, 1), -1e30, F32))

    def mix(i, carry):
        total, acc = carry
        p = jnp.exp(scores[i] - top)
        values = lat[pl.ds(i * 2, 2), :, :KV_RANK].reshape(256, KV_RANK)
        return total + jnp.sum(p, axis=1, keepdims=True), acc + dot(p.astype(BF), values)

    total, acc = lax.fori_loop(
        0, 8, mix, (jnp.zeros((128, 1), F32), jnp.zeros((128, KV_RANK), F32))
    )
    attn_ref[...] = (acc / total).astype(BF)

    wait(back.at[pl.ds(0, 63)], rt_r)
    rows = back[...].astype(F32).reshape(512, 128).astype(BF)
    mixed = dot(comb_hi[...], rows, ((0,), (0,))) + dot(comb_lo[...], rows, ((0,), (0,)))
    for j in range(4):
        width = min(128, 448 - 128 * j)
        moe_ref[:, 128 * j : 128 * j + width] = mixed[8 * j : 8 * j + 8, :width].astype(BF)

    wait(hall.at[0, 0, pl.ds(0, 3)], hx_s)
    wait(hall.at[0, pl.ds(0, 7)], hz_s)
    wait(hall.at[0], hc_s)
    wait(part.at[pl.ds(0, 8)], rx_s)
    wait(part.at[pl.ds(0, 7)], ry_s)
    wait(inner.at[pl.ds(0, 7)], ay_s)
    wait(inner.at[pl.ds(0, 8)], ax_s)
    wait(ret.at[pl.ds(0, 63)], rt_s)
    wait(lat.at[pl.ds(0, 7), pl.ds(0, 64)], ly_s)
    wait(own_half, lx_s)
    wait(own_half, lc_s.at[0])
    wait(own_half, lc_s.at[1])


def per_device(queries, latents, group_order, hidden_b, expert_ids, gate_fixed, w_gate, w_up, w_down):
    hbm = pl.BlockSpec(memory_space=pl.ANY)
    vmem = pl.BlockSpec(memory_space=pltpu.VMEM)
    dma = pltpu.SemaphoreType.DMA
    return pl.pallas_call(
        kernel,
        out_shape=(
            jax.ShapeDtypeStruct((128, 512), BF),
            jax.ShapeDtypeStruct((8, 448), BF),
        ),
        in_specs=[hbm, hbm, vmem, vmem, vmem, vmem, hbm, hbm, hbm],
        out_specs=(vmem, vmem),
        scratch_shapes=[
            pltpu.VMEM((128, 576), BF),
            pltpu.VMEM((16, 128, 576), BF),
            pltpu.VMEM((512, 1024), BF),
            pltpu.VMEM((512, 1024), BF),
            pltpu.VMEM((1024, 448), BF),
            pltpu.VMEM((8, 512), F32),
            pltpu.VMEM((2, 8, 4, 16, 256), BF),
            pltpu.VMEM((16, 16, 1024), BF),
            pltpu.VMEM((8, 16, 1024), BF),
            pltpu.VMEM((8, 16, 1024), BF),
            pltpu.VMEM((16, 16, 512), BF),
            pltpu.VMEM((128, 512), F32),
            pltpu.VMEM((64, 8, 128), BF),
            pltpu.VMEM((64, 8, 128), BF),
            pltpu.VMEM((512, 32), BF),
            pltpu.VMEM((512, 32), BF),
            pltpu.VMEM((8, 128, 256), F32),
            dma((3,)), dma, dma,
            dma, dma, dma, dma((8,)), dma, dma,
            dma, dma((8,)), dma, dma,
            dma, dma((8,)), dma, dma,
            dma, dma,
            dma, dma, dma, dma, dma((2,)), dma((2,)),
        ],
        compiler_params=pltpu.CompilerParams(
            collective_id=0, has_side_effects=True, vmem_limit_bytes=32 << 20
        ),
        name="layer",
    )(
        queries, latents, group_order.reshape(1, 64), hidden_b, expert_ids, gate_fixed,
        w_gate, w_up, w_down,
    )


def solution(mesh):
    in_specs = (
        P("ctx", "exp"),
        P("ctx", None),
        P(),
        P("exp", "ctx"),
        P("exp", None),
        P("exp", None),
        P("exp", "ctx", None),
        P("exp", "ctx", None),
        P("exp", None, "ctx"),
    )
    out_specs = (P("ctx", "exp"), P("exp", "ctx"))
    return jax.shard_map(
        per_device, mesh=mesh, in_specs=in_specs, out_specs=out_specs, check_vma=False
    )
```

```python
import functools
import math

import jax
import jax.numpy as jnp
from jax import lax
from jax.experimental import pallas as pl
from jax.experimental.pallas import tpu as pltpu
from jax.sharding import PartitionSpec as P

MESH = pl.DeviceIdType.MESH
SCALE = 1.0 / math.sqrt(192.0)
KV_RANK = 512
BF = jnp.bfloat16
F32 = jnp.float32
I32 = jnp.int32


def iota(shape, dim):
    return lax.broadcasted_iota(I32, shape, dim)


def dot(a, b, dims=((1,), (0,))):
    return lax.dot_general(a, b, (dims, ((), ())), preferred_element_type=F32)


def kernel(
    q_hbm, lat_hbm, go_hbm, hid_hbm, ids_hbm, gate_hbm, wg_hbm, wu_hbm, wd_hbm,
    attn_ref, moe_ref,
    q, lat, wg, wu, wd, go_v, hid_v, ids_v, gate_v, pay, hall, part, own_part, xin, yin, inner, zbuf, ret, back, comb_hi, comb_lo, scores,
    wsem, qsem, lsem, tsem, near, ready, hx_s, hx_r, hz_s, hz_r, hc_s, hc_r,
    rx_s, rx_r, ry_s, ry_r, ay_s, ay_r, ax_s, ax_r, rt_s, rt_r,
    ly_s, ly_r, lz_s, lz_r, lx_s, lx_r, lc_s, lc_r,
):
    c = lax.axis_index("ctx")
    e = lax.axis_index("exp")
    xl, y = c // 8, c % 8
    xh, z, core = e // 16, (e // 2) % 8, e % 2

    def dev(c_, e_):
        return {"ctx": c_, "exp": e_}

    def exp_at(xh_, z_, core_):
        return (xh_ * 8 + z_) * 2 + core_

    def x_peer(k):
        return dev(c, exp_at((xh + k) % 4, z, core))

    def z_peer(k):
        return dev(c, exp_at(xh, (z + k) % 8, core))

    def y_peer(k):
        return dev(xl * 8 + (y + k) % 8, e)

    shift = jnp.where((c == 0) & (e // 16 == 0) & (core == 0), 1, 0)
    turn = (z + 8 - shift) % 8

    def z_at(t):
        return (t + shift) % 8

    def column(t):
        return dev(c, exp_at(xh, z_at(t), core))

    sibling = dev(c, exp_at(xh, z, 1 - core))
    pair = dev((c + 8) % 16, e)
    far_pair = dev((c + 8) % 16, exp_at((xh + 3 + 2 * xl) % 4, z, core))

    def send(src, dst, ss, rs, to):
        pltpu.make_async_remote_copy(
            src_ref=src, dst_ref=dst, send_sem=ss, recv_sem=rs, device_id=to, device_id_type=MESH
        ).start()

    def wait(like, sem):
        pltpu.make_async_copy(like, like, sem).wait()

    barrier = pltpu.get_barrier_semaphore()

    def hello(to, sem=barrier):
        pl.semaphore_signal(sem, inc=1, device_id=to, device_id_type=MESH)

    for to in (x_peer(1), x_peer(3), sibling, pair, far_pair, y_peer(1), y_peer(7)):
        hello(to)

    @pl.loop(turn + 1, 8)
    def _(t):
        hello(column(t))

    small_copies = [
        pltpu.make_async_copy(src, dst, tsem.at[n])
        for n, (src, dst) in enumerate(
            ((hid_hbm, hid_v), (ids_hbm, ids_v), (gate_hbm, gate_v), (go_hbm, go_v))
        )
    ]
    for cp in small_copies:
        cp.start()
    half = pl.ds(pl.multiple_of(core * 288, 16), 288)
    lat_copy = pltpu.make_async_copy(lat_hbm.at[half], lat.at[c, half], lsem)
    late = z >= 6

    @pl.when(z < 6)
    def _():
        lat_copy.start()

    w_copies = [
        pltpu.make_async_copy(wg_hbm.at[0], wg.at[pl.ds(0, 448)], wsem.at[0]),
        pltpu.make_async_copy(wu_hbm.at[0], wu.at[pl.ds(0, 448)], wsem.at[1]),
        pltpu.make_async_copy(wd_hbm.at[0], wd, wsem.at[2]),
    ]
    for cp in w_copies:
        cp.start()
    q_copy = pltpu.make_async_copy(q_hbm, q, qsem)
    q_copy.start()

    for cp in small_copies:
        cp.wait()
    ids = ids_v[...].astype(F32)
    pay[...] = jnp.zeros((8, 512), F32)
    pay[:, :448] = hid_v[...].astype(F32)
    spread = (iota((8, 128), 1) == iota((8, 128), 0) + 64).astype(BF)
    pay[:, 384:] = pay[:, 384:] + dot(ids.astype(BF), spread)
    hall[core, z, xh] = jnp.concatenate([pay[:, :256], pay[:, 256:]], axis=0).astype(BF)
    for w in (wg, wu):
        w[448:, :] = jnp.zeros((64, 1024), BF)
    zbuf[:, 384:] = jnp.zeros((128, 128), F32)

    pl.semaphore_wait(barrier, 7 + turn)

    @pl.loop(0, turn)
    def _(t):
        hello(column(t), ready.at[turn])

    def greet_y(n):
        hello(y_peer(1), near.at[n, 0])
        hello(y_peer(7), near.at[n, 1])

    def greeted_y(n):
        pl.semaphore_wait(near.at[n, 0], 1)
        pl.semaphore_wait(near.at[n, 1], 1)

    mine = hall.at[core, z, xh]
    send(mine, mine, hx_s, hx_r.at[0], x_peer(1))
    send(mine, mine, hx_s, hx_r.at[1], x_peer(3))
    greet_y(0)
    before_me = hall.at[core, z, (xh + 3) % 4]
    wait(before_me, hx_r.at[0])
    send(before_me, before_me, hx_s, hx_r.at[2], x_peer(1))
    greeted_y(0)
    greet_y(1)
    wait(mine, hx_r.at[1])
    wait(mine, hx_r.at[2])

    slab = hall.at[core, z]

    @pl.loop(0, turn)
    def _(t):
        send(slab, slab, hz_s, hz_r.at[turn], column(t))

    send(slab, slab, hc_s, hc_r, sibling)
    greeted_y(1)
    greet_y(2)

    @pl.when(z < 6)
    def _():
        greeted_y(2)
        lat_copy.wait()

        @pl.loop(1, 8)
        def _(k):
            block = lat.at[c, half]
            send(block, block, ly_s, ly_r, y_peer(k))

    @pl.loop(turn + 1, 8)
    def _(t):
        pl.semaphore_wait(ready.at[t], 1)
        send(slab, slab, hz_s, hz_r.at[turn], column(t))

    @pl.when(late)
    def _():
        greeted_y(2)

    @pl.loop(0, 7)
    def _(n):
        t = jnp.where(n < turn, (n % 2) * (n // 2) + (1 - n % 2) * (turn - 1 - n // 2), n + 1)
        from_z = hall.at[core, z_at(t)]
        wait(from_z, hz_r.at[t])
        send(from_z, from_z, hc_s, hc_r, sibling)

    wait(hall.at[1 - core], hc_r)

    rows2d = hall[...].reshape(1024, 256)
    id_lane = iota((1024, 128), 1)
    named = jnp.where(
        (rows2d[:, 128:].astype(F32) == e.astype(F32)) & (id_lane >= 64) & (id_lane < 72), 1.0, 0.0
    ).astype(BF)
    hit = dot(jnp.ones((8, 128), BF), named, ((1,), (1,)))
    col = iota((8, 1024), 1)
    tok = col % 8
    hit = jnp.where((col // 8) % 2 == 1, hit, 0.0)
    upto = hit
    for step in (1, 2, 4):
        upto = upto + jnp.where(tok >= step, pltpu.roll(upto, step, 1), 0.0)
    code = jnp.where(hit > 0.5, (col // 16).astype(F32) * 2.0 + upto - hit, -1.0)
    row_id = iota((128, 1024), 0).astype(F32)
    pick_hi = jnp.where(code[:1] == row_id, 1.0, 0.0).astype(BF)
    pick_lo = jnp.where(pltpu.roll(code, 1024 - 8, 1)[:1] == row_id, 1.0, 0.0).astype(BF)
    x_lo = dot(pick_lo, rows2d).astype(BF)
    x_hi = dot(pick_hi, rows2d).astype(BF)

    w_copies[0].wait()
    w_copies[1].wait()

    def far_first(n):
        return 4 + (1 - 2 * (n % 2)) * ((n + 1) // 2)

    other = (1 - xl) * 8

    for h in range(2):
        units = slice(512 * h, 512 * (h + 1))
        gate_part = dot(x_lo, wg[:256, units]) + dot(x_hi, wg[256:, units])
        up_part = dot(x_lo, wu[:256, units]) + dot(x_hi, wu[256:, units])
        own_part[h] = jnp.concatenate(
            [gate_part.reshape(16, 8, 512), up_part.reshape(16, 8, 512)], axis=1
        )
        part[h] = own_part[h].astype(BF)

        @pl.loop(0, 8)
        def _(n):
            send(
                part.at[h, other + (y + far_first(n)) % 8], xin.at[h, n],
                rx_s.at[h], rx_r.at[h, n], pair,
            )

    own_half = lat.at[pl.ds(xl * 8, 8), half]
    other_half = lat.at[pl.ds(other, 8), half]

    def latents_along_x():
        send(own_half, own_half, lx_s, lx_r, far_pair)
        send(own_half, own_half, lc_s.at[0], lc_r.at[0], sibling)

    def latents_across():
        wait(own_half, lx_r)
        send(other_half, other_half, lc_s.at[1], lc_r.at[1], sibling)

    @pl.when(z < 6)
    def _():
        wait(lat.at[pl.ds(0, 7), pl.ds(0, 288)], ly_r)
        latents_along_x()

    @pl.when((z == 0) | (z == 5))
    def _():
        to_late = dev(c, exp_at(xh, jnp.where(z == 0, 7, 6), core))
        send(own_half, own_half, lz_s, lz_r, to_late)

    def add_pair(h, n):
        own = xl * 8 + (y + far_first(n)) % 8
        wait(xin.at[h, n], rx_r.at[h, n])
        return own, own_part[h, own] + xin[h, n].astype(F32)

    own_totals = []
    for h in range(2):
        @pl.loop(0, 7)
        def _(n):
            own, total = add_pair(h, n)
            part[h, own] = total.astype(BF)
            send(part.at[h, own], yin.at[h, y], ry_s.at[h], ry_r.at[h], y_peer(far_first(n)))

        own_totals.append(add_pair(h, 7)[1])
        yin[h, y] = jnp.zeros((16, 512), BF)

    for h in range(2):
        wait(yin.at[h, pl.ds(0, 7)], ry_r.at[h])
        summed = own_totals[h] + jnp.sum(yin[h].astype(F32), axis=0)
        gate_sum, up_sum = summed[:8], summed[8:]
        act = gate_sum / (1.0 + jnp.exp(-gate_sum)) * up_sum
        inner[h, c] = jnp.concatenate([act[:, :256], act[:, 256:]], axis=0).astype(BF)
        own_act = inner.at[h, c]

        @pl.loop(0, 8)
        def _(n):
            k = far_first(n)
            send(own_act, own_act, ax_s.at[h], ax_r.at[h], dev(other + (y + k) % 8, e))

            @pl.when(n < 7)
            def _():
                send(own_act, own_act, ay_s.at[h], ay_r.at[h], y_peer(k))

    @pl.when(z < 6)
    def _():
        latents_across()

    @pl.when(late)
    def _():
        wait(own_half, lz_r)
        latents_along_x()

    w_copies[2].wait()
    result = jnp.zeros((128, 448), F32)
    for h in range(2):
        wait(inner.at[h, pl.ds(0, 7)], ay_r.at[h])
        wait(inner.at[h, pl.ds(0, 8)], ax_r.at[h])
        acts = inner[h].astype(F32)
        for u, rows in enumerate((acts[:, :8], acts[:, 8:])):
            first = 512 * h + 256 * u
            result = result + dot(
                rows.reshape(128, 256).astype(BF), wd[:, first : first + 256], ((1,), (1,))
            )
    zbuf[:, :448] = result
    out_row = iota((512, 128), 0)
    in_row = iota((512, 128), 1)
    packed = jnp.zeros((512, 128), F32)
    for j in range(4):
        place = jnp.where(out_row == 4 * in_row + j, 1.0, 0.0).astype(BF)
        packed = packed + dot(place, zbuf[:, 128 * j : 128 * (j + 1)].astype(BF))
    ret[...] = packed.reshape(64, 8, 128).astype(BF)

    me = (core * 8 + z) * 4 + xh

    @pl.loop(0, 63)
    def _(n):
        m = n % 8 // 2
        to_z = (z + far_first(n // 8)) % 8
        to_x = (xh + 2 + (1 - 2 * (m % 2)) * ((m + 1) // 2)) % 4
        to_core = (core + 1 - n % 2) % 2
        g = (to_core * 8 + to_z) * 4 + to_x
        send(ret.at[g], back.at[me], rt_s, rt_r, dev(c, exp_at(to_x, to_z, to_core)))

    back[me] = ret[me]

    @pl.when(late)
    def _():
        latents_across()

    r_id = iota((512, 32), 0)
    q_id = iota((512, 32), 1)
    grp = r_id // 8
    expert_of_row = (((grp % 4) * 8 + (grp // 4) % 8) * 2 + grp // 32).astype(F32)
    diag = iota((8, 32), 0) == iota((8, 32), 1) % 8
    gates = gate_v[...].astype(F32)
    found = jnp.zeros((512, 32), F32)
    gated = jnp.zeros((512, 32), F32)
    for k in range(8):
        id_row = jnp.sum(jnp.where(diag, ids[:, k : k + 1], 0.0), axis=0, keepdims=True)
        gate_row = jnp.sum(jnp.where(diag, gates[:, k : k + 1], 0.0), axis=0, keepdims=True)
        same = expert_of_row == id_row
        found = found + jnp.where(same, 1.0, 0.0)
        gated = gated + jnp.where(same, gate_row, 0.0)
    a_id, b_id = iota((32, 32), 0), iota((32, 32), 1)
    earlier = jnp.where((a_id // 8 == b_id // 8) & (a_id < b_id), 1.0, 0.0).astype(BF)
    before = dot(found.astype(BF), earlier)
    mine = (
        (found > 0.5) & (before == ((r_id // 4) % 2).astype(F32)) & (r_id % 4 == q_id // 8)
    )
    weight = jnp.where(mine, gated * (1.0 / 32768.0), 0.0)
    weight_hi = weight.astype(BF)
    comb_hi[...] = weight_hi
    comb_lo[...] = (weight - weight_hi.astype(F32)).astype(BF)

    go = go_v[...].astype(F32)
    blk = iota((128, 64), 1)
    own_blk = c * 4 + iota((128, 64), 0) // 32
    query_pos = jnp.sum(jnp.where(blk == own_blk, go, 0.0), axis=1, keepdims=True) * 32.0 + (
        iota((128, 1), 0) % 32
    ).astype(F32)
    wait(own_half, lc_r.at[0])
    wait(own_half, lc_r.at[1])
    q_copy.wait()
    eye = jnp.where(iota((128, 128), 0) == iota((128, 128), 1), 1.0, 0.0).astype(BF)
    queries = dot(eye, q[...], ((1,), (1,))).astype(BF)

    def score(i, top):
        keys = jnp.concatenate([lat[2 * i], lat[2 * i + 1]], axis=1)
        lane = iota((64, 256), 1)
        owner = jnp.where(iota((64, 256), 0) == i * 8 + lane // 32, 1.0, 0.0).astype(BF)
        base = dot(go.astype(BF), owner)
        key_pos = base * 32.0 + (iota((1, 256), 1) % 32).astype(F32)
        s = dot(queries, keys) * SCALE
        s = jnp.where(key_pos <= query_pos, s, -1e30)
        scores[i] = s
        return jnp.maximum(top, jnp.max(s, axis=1, keepdims=True))

    top = lax.fori_loop(0, 8, score, jnp.full((128, 1), -1e30, F32))

    def mix(i, carry):
        total, acc = carry
        p = jnp.exp(scores[i] - top)
        values = jnp.concatenate([lat[2 * i, :KV_RANK], lat[2 * i + 1, :KV_RANK]], axis=1)
        return total + jnp.sum(p, axis=1, keepdims=True), acc + dot(p.astype(BF), values, ((1,), (1,)))

    total, acc = lax.fori_loop(
        0, 8, mix, (jnp.zeros((128, 1), F32), jnp.zeros((128, KV_RANK), F32))
    )
    attn_ref[...] = (acc / total).astype(BF)

    wait(back.at[pl.ds(0, 63)], rt_r)
    rows = back[...].astype(F32).reshape(512, 128).astype(BF)
    mixed = dot(comb_hi[...], rows, ((0,), (0,))) + dot(comb_lo[...], rows, ((0,), (0,)))
    for j in range(4):
        width = min(128, 448 - 128 * j)
        moe_ref[:, 128 * j : 128 * j + width] = mixed[8 * j : 8 * j + 8, :width].astype(BF)

    wait(hall.at[0, 0, pl.ds(0, 3)], hx_s)
    wait(hall.at[0, pl.ds(0, 7)], hz_s)
    wait(hall.at[0], hc_s)
    for h in range(2):
        wait(part.at[h, pl.ds(0, 8)], rx_s.at[h])
        wait(part.at[h, pl.ds(0, 7)], ry_s.at[h])
        wait(inner.at[h, pl.ds(0, 7)], ay_s.at[h])
        wait(inner.at[h, pl.ds(0, 8)], ax_s.at[h])
    wait(ret.at[pl.ds(0, 63)], rt_s)
    @pl.when(z < 6)
    def _():
        wait(lat.at[pl.ds(0, 7), pl.ds(0, 288)], ly_s)

    @pl.when((z == 0) | (z == 5))
    def _():
        wait(own_half, lz_s)

    wait(own_half, lx_s)
    wait(own_half, lc_s.at[0])
    wait(own_half, lc_s.at[1])


def per_device(queries, latents, group_order, hidden_b, expert_ids, gate_fixed, w_gate, w_up, w_down):
    hbm = pl.BlockSpec(memory_space=pltpu.HBM)
    vmem = pl.BlockSpec(memory_space=pltpu.VMEM)
    dma = pltpu.SemaphoreType.DMA
    return pl.pallas_call(
        kernel,
        out_shape=(
            pltpu.VMEM((128, 512), BF),
            pltpu.VMEM((8, 448), BF),
        ),
        in_specs=[hbm] * 9,
        out_specs=(vmem, vmem),
        scratch_shapes=[
            pltpu.VMEM((576, 128), BF),
            pltpu.VMEM((16, 576, 128), BF),
            pltpu.VMEM((512, 1024), BF),
            pltpu.VMEM((512, 1024), BF),
            pltpu.VMEM((448, 1024), BF),
            pltpu.VMEM((1, 64), I32),
            pltpu.VMEM((8, 448), BF),
            pltpu.VMEM((8, 8), I32),
            pltpu.VMEM((8, 8), I32),
            pltpu.VMEM((8, 512), F32),
            pltpu.VMEM((2, 8, 4, 16, 256), BF),
            pltpu.VMEM((2, 16, 16, 512), BF),
            pltpu.VMEM((2, 16, 16, 512), F32),
            pltpu.VMEM((2, 8, 16, 512), BF),
            pltpu.VMEM((2, 8, 16, 512), BF),
            pltpu.VMEM((2, 16, 16, 256), BF),
            pltpu.VMEM((128, 512), F32),
            pltpu.VMEM((64, 8, 128), BF),
            pltpu.VMEM((64, 8, 128), BF),
            pltpu.VMEM((512, 32), BF),
            pltpu.VMEM((512, 32), BF),
            pltpu.VMEM((8, 128, 256), F32),
            dma((3,)), dma, dma, dma((4,)),
            pltpu.SemaphoreType.REGULAR((3, 2)),
            pltpu.SemaphoreType.REGULAR((8,)),
            dma, dma((3,)), dma, dma((8,)), dma, dma,
            dma((2,)), dma((2, 8)), dma((2,)), dma((2,)),
            dma((2,)), dma((2,)), dma((2,)), dma((2,)),
            dma, dma,
            dma, dma, dma, dma, dma, dma, dma((2,)), dma((2,)),
        ],
        compiler_params=pltpu.CompilerParams(
            collective_id=0, has_side_effects=True, vmem_limit_bytes=60 << 20
        ),
        name="layer",
    )(
        queries.T, latents.T, group_order.reshape(1, 64), hidden_b, expert_ids, gate_fixed,
        w_gate, w_up, jnp.swapaxes(w_down, 1, 2),
    )


def solution(mesh):
    in_specs = (
        P("ctx", "exp"),
        P("ctx", None),
        P(),
        P("exp", "ctx"),
        P("exp", None),
        P("exp", None),
        P("exp", "ctx", None),
        P("exp", "ctx", None),
        P("exp", None, "ctx"),
    )
    out_specs = (P("ctx", "exp"), P("exp", "ctx"))
    return jax.shard_map(
        per_device, mesh=mesh, in_specs=in_specs, out_specs=out_specs, check_vma=False
    )
```

```python
import functools
import math

import jax
import jax.numpy as jnp
from jax import lax
from jax.experimental import pallas as pl
from jax.experimental.pallas import tpu as pltpu
from jax.sharding import PartitionSpec as P

MESH = pl.DeviceIdType.MESH
SCALE = 1.0 / math.sqrt(192.0)
KV_RANK = 512
BF = jnp.bfloat16
F32 = jnp.float32
I32 = jnp.int32


def iota(shape, dim):
    return lax.broadcasted_iota(I32, shape, dim)


def dot(a, b, dims=((1,), (0,))):
    return lax.dot_general(a, b, (dims, ((), ())), preferred_element_type=F32)


def kernel(
    q_hbm, lat_hbm, go_hbm, hid_hbm, ids_hbm, gate_hbm, wg_hbm, wu_hbm, wd_hbm,
    attn_ref, moe_ref,
    q, lat, wg, wu, wd, go_v, hid_v, ids_v, gate_v, pay, hall, part, own_part, xin, yin, inner, zbuf, ret, back, comb_hi, comb_lo, scores,
    wsem, qsem, lsem, tsem, near, ready, hx_s, hx_r, hz_s, hz_r, hc_s, hc_r,
    rx_s, rx_r, ry_s, ry_r, ay_s, ay_r, ax_s, ax_r, rt_s, rt_r,
    ly_s, ly_r, lx_s, lx_r, lc_s, lc_r,
):
    c = lax.axis_index("ctx")
    e = lax.axis_index("exp")
    xl, y = c // 8, c % 8
    xh, z, core = e // 16, (e // 2) % 8, e % 2

    def dev(c_, e_):
        return {"ctx": c_, "exp": e_}

    def exp_at(xh_, z_, core_):
        return (xh_ * 8 + z_) * 2 + core_

    def x_peer(k):
        return dev(c, exp_at((xh + k) % 4, z, core))

    def z_peer(k):
        return dev(c, exp_at(xh, (z + k) % 8, core))

    def y_peer(k):
        return dev(xl * 8 + (y + k) % 8, e)

    shift = jnp.where((c == 0) & (e // 16 == 0) & (core == 0), 1, 0)
    turn = (z + 8 - shift) % 8

    def z_at(t):
        return (t + shift) % 8

    def column(t):
        return dev(c, exp_at(xh, z_at(t), core))

    sibling = dev(c, exp_at(xh, z, 1 - core))
    pair = dev((c + 8) % 16, e)
    far_pair = dev((c + 8) % 16, exp_at((xh + 3 + 2 * xl) % 4, z, core))

    def send(src, dst, ss, rs, to):
        pltpu.make_async_remote_copy(
            src_ref=src, dst_ref=dst, send_sem=ss, recv_sem=rs, device_id=to, device_id_type=MESH
        ).start()

    def wait(like, sem):
        pltpu.make_async_copy(like, like, sem).wait()

    barrier = pltpu.get_barrier_semaphore()

    def hello(to, sem=barrier):
        pl.semaphore_signal(sem, inc=1, device_id=to, device_id_type=MESH)

    for to in (x_peer(1), x_peer(3), sibling, pair, far_pair, y_peer(1), y_peer(7)):
        hello(to)

    @pl.loop(turn + 1, 8)
    def _(t):
        hello(column(t))

    small_copies = [
        pltpu.make_async_copy(src, dst, tsem.at[n])
        for n, (src, dst) in enumerate(
            ((hid_hbm, hid_v), (ids_hbm, ids_v), (gate_hbm, gate_v), (go_hbm, go_v))
        )
    ]
    for cp in small_copies:
        cp.start()
    half = pl.ds(pl.multiple_of(core * 288, 16), 288)
    lat_copy = pltpu.make_async_copy(lat_hbm.at[half], lat.at[c, half], lsem)
    lat_copy.start()
    w_copies = [
        pltpu.make_async_copy(wg_hbm.at[0], wg.at[pl.ds(0, 448)], wsem.at[0]),
        pltpu.make_async_copy(wu_hbm.at[0], wu.at[pl.ds(0, 448)], wsem.at[1]),
        pltpu.make_async_copy(wd_hbm.at[0], wd, wsem.at[2]),
    ]
    for cp in w_copies:
        cp.start()
    q_copy = pltpu.make_async_copy(q_hbm, q, qsem)
    q_copy.start()

    for cp in small_copies:
        cp.wait()
    ids = ids_v[...].astype(F32)
    pay[...] = jnp.zeros((8, 512), F32)
    pay[:, :448] = hid_v[...].astype(F32)
    spread = (iota((8, 128), 1) == iota((8, 128), 0) + 64).astype(BF)
    pay[:, 384:] = pay[:, 384:] + dot(ids.astype(BF), spread)
    hall[core, z, xh] = jnp.concatenate([pay[:, :256], pay[:, 256:]], axis=0).astype(BF)
    for w in (wg, wu):
        w[448:, :] = jnp.zeros((64, 1024), BF)
    zbuf[:, 384:] = jnp.zeros((128, 128), F32)

    pl.semaphore_wait(barrier, 7 + turn)

    @pl.loop(0, turn)
    def _(t):
        hello(column(t), ready.at[turn])

    def greet_y(n):
        hello(y_peer(1), near.at[n, 0])
        hello(y_peer(7), near.at[n, 1])

    def greeted_y(n):
        pl.semaphore_wait(near.at[n, 0], 1)
        pl.semaphore_wait(near.at[n, 1], 1)

    mine = hall.at[core, z, xh]
    send(mine, mine, hx_s, hx_r.at[0], x_peer(1))
    send(mine, mine, hx_s, hx_r.at[1], x_peer(3))
    greet_y(0)
    before_me = hall.at[core, z, (xh + 3) % 4]
    wait(before_me, hx_r.at[0])
    send(before_me, before_me, hx_s, hx_r.at[2], x_peer(1))
    greeted_y(0)
    greet_y(1)
    wait(mine, hx_r.at[1])
    wait(mine, hx_r.at[2])

    slab = hall.at[core, z]

    @pl.loop(0, turn)
    def _(t):
        send(slab, slab, hz_s, hz_r.at[turn], column(t))

    send(slab, slab, hc_s, hc_r, sibling)
    greeted_y(1)
    greet_y(2)
    lat_copy.wait()

    def latents_along_y():
        greeted_y(2)

        @pl.loop(1, 8)
        def _(k):
            block = lat.at[c, half]
            send(block, block, ly_s, ly_r, y_peer(k))

    @pl.when(z < 6)
    def _():
        latents_along_y()

    @pl.loop(turn + 1, 8)
    def _(t):
        pl.semaphore_wait(ready.at[t], 1)
        send(slab, slab, hz_s, hz_r.at[turn], column(t))

    @pl.when(z >= 6)
    def _():
        latents_along_y()

    @pl.loop(0, 7)
    def _(n):
        t = jnp.where(n < turn, (n % 2) * (n // 2) + (1 - n % 2) * (turn - 1 - n // 2), n + 1)
        from_z = hall.at[core, z_at(t)]
        wait(from_z, hz_r.at[t])
        send(from_z, from_z, hc_s, hc_r, sibling)

    wait(hall.at[1 - core], hc_r)

    rows2d = hall[...].reshape(1024, 256)
    id_lane = iota((1024, 128), 1)
    named = jnp.where(
        (rows2d[:, 128:].astype(F32) == e.astype(F32)) & (id_lane >= 64) & (id_lane < 72), 1.0, 0.0
    ).astype(BF)
    hit = dot(jnp.ones((8, 128), BF), named, ((1,), (1,)))
    col = iota((8, 1024), 1)
    tok = col % 8
    hit = jnp.where((col // 8) % 2 == 1, hit, 0.0)
    upto = hit
    for step in (1, 2, 4):
        upto = upto + jnp.where(tok >= step, pltpu.roll(upto, step, 1), 0.0)
    code = jnp.where(hit > 0.5, (col // 16).astype(F32) * 2.0 + upto - hit, -1.0)
    row_id = iota((128, 1024), 0).astype(F32)
    pick_hi = jnp.where(code[:1] == row_id, 1.0, 0.0).astype(BF)
    pick_lo = jnp.where(pltpu.roll(code, 1024 - 8, 1)[:1] == row_id, 1.0, 0.0).astype(BF)
    x_lo = dot(pick_lo, rows2d).astype(BF)
    x_hi = dot(pick_hi, rows2d).astype(BF)

    w_copies[0].wait()
    w_copies[1].wait()

    def far_first(n):
        return 4 + (1 - 2 * (n % 2)) * ((n + 1) // 2)

    other = (1 - xl) * 8

    for h in range(2):
        units = slice(512 * h, 512 * (h + 1))
        gate_part = dot(x_lo, wg[:256, units]) + dot(x_hi, wg[256:, units])
        up_part = dot(x_lo, wu[:256, units]) + dot(x_hi, wu[256:, units])
        own_part[h] = jnp.concatenate(
            [gate_part.reshape(16, 8, 512), up_part.reshape(16, 8, 512)], axis=1
        )
        part[h] = own_part[h].astype(BF)

        @pl.loop(0, 8)
        def _(n):
            send(
                part.at[h, other + (y + far_first(n)) % 8], xin.at[h, n],
                rx_s.at[h], rx_r.at[h, n], pair,
            )

    own_half = lat.at[pl.ds(xl * 8, 8), half]
    other_half = lat.at[pl.ds(other, 8), half]

    def latents_along_x():
        wait(lat.at[pl.ds(0, 7), pl.ds(0, 288)], ly_r)
        send(own_half, own_half, lx_s, lx_r, far_pair)
        send(own_half, own_half, lc_s.at[0], lc_r.at[0], sibling)

    def latents_across():
        wait(own_half, lx_r)
        send(other_half, other_half, lc_s.at[1], lc_r.at[1], sibling)

    @pl.when(z < 6)
    def _():
        latents_along_x()

    def add_pair(h, n):
        own = xl * 8 + (y + far_first(n)) % 8
        wait(xin.at[h, n], rx_r.at[h, n])
        return own, own_part[h, own] + xin[h, n].astype(F32)

    own_totals = []
    for h in range(2):
        @pl.loop(0, 7)
        def _(n):
            own, total = add_pair(h, n)
            part[h, own] = total.astype(BF)
            send(part.at[h, own], yin.at[h, y], ry_s.at[h], ry_r.at[h], y_peer(far_first(n)))

        own_totals.append(add_pair(h, 7)[1])
        yin[h, y] = jnp.zeros((16, 512), BF)

    @pl.when(z >= 6)
    def _():
        latents_along_x()

    for h in range(2):
        wait(yin.at[h, pl.ds(0, 7)], ry_r.at[h])
        summed = own_totals[h] + jnp.sum(yin[h].astype(F32), axis=0)
        gate_sum, up_sum = summed[:8], summed[8:]
        act = gate_sum / (1.0 + jnp.exp(-gate_sum)) * up_sum
        inner[h, c] = jnp.concatenate([act[:, :256], act[:, 256:]], axis=0).astype(BF)
        own_act = inner.at[h, c]

        @pl.loop(0, 8)
        def _(n):
            k = far_first(n)
            send(own_act, own_act, ax_s.at[h], ax_r.at[h], dev(other + (y + k) % 8, e))

            @pl.when(n < 7)
            def _():
                send(own_act, own_act, ay_s.at[h], ay_r.at[h], y_peer(k))

    @pl.when(z < 6)
    def _():
        latents_across()

    w_copies[2].wait()
    result = jnp.zeros((128, 448), F32)
    for h in range(2):
        wait(inner.at[h, pl.ds(0, 7)], ay_r.at[h])
        wait(inner.at[h, pl.ds(0, 8)], ax_r.at[h])
        acts = inner[h].astype(F32)
        for u, rows in enumerate((acts[:, :8], acts[:, 8:])):
            first = 512 * h + 256 * u
            result = result + dot(
                rows.reshape(128, 256).astype(BF), wd[:, first : first + 256], ((1,), (1,))
            )
    zbuf[:, :448] = result
    out_row = iota((512, 128), 0)
    in_row = iota((512, 128), 1)
    packed = jnp.zeros((512, 128), F32)
    for j in range(4):
        place = jnp.where(out_row == 4 * in_row + j, 1.0, 0.0).astype(BF)
        packed = packed + dot(place, zbuf[:, 128 * j : 128 * (j + 1)].astype(BF))
    ret[...] = packed.reshape(64, 8, 128).astype(BF)

    me = (core * 8 + z) * 4 + xh

    @pl.loop(0, 63)
    def _(n):
        m = n % 8 // 2
        to_z = (z + far_first(n // 8)) % 8
        to_x = (xh + 2 + (1 - 2 * (m % 2)) * ((m + 1) // 2)) % 4
        to_core = (core + 1 - n % 2) % 2
        g = (to_core * 8 + to_z) * 4 + to_x
        send(ret.at[g], back.at[me], rt_s, rt_r, dev(c, exp_at(to_x, to_z, to_core)))

    back[me] = ret[me]

    @pl.when(z >= 6)
    def _():
        latents_across()

    r_id = iota((512, 32), 0)
    q_id = iota((512, 32), 1)
    grp = r_id // 8
    expert_of_row = (((grp % 4) * 8 + (grp // 4) % 8) * 2 + grp // 32).astype(F32)
    diag = iota((8, 32), 0) == iota((8, 32), 1) % 8
    gates = gate_v[...].astype(F32)
    found = jnp.zeros((512, 32), F32)
    gated = jnp.zeros((512, 32), F32)
    for k in range(8):
        id_row = jnp.sum(jnp.where(diag, ids[:, k : k + 1], 0.0), axis=0, keepdims=True)
        gate_row = jnp.sum(jnp.where(diag, gates[:, k : k + 1], 0.0), axis=0, keepdims=True)
        same = expert_of_row == id_row
        found = found + jnp.where(same, 1.0, 0.0)
        gated = gated + jnp.where(same, gate_row, 0.0)
    a_id, b_id = iota((32, 32), 0), iota((32, 32), 1)
    earlier = jnp.where((a_id // 8 == b_id // 8) & (a_id < b_id), 1.0, 0.0).astype(BF)
    before = dot(found.astype(BF), earlier)
    mine = (
        (found > 0.5) & (before == ((r_id // 4) % 2).astype(F32)) & (r_id % 4 == q_id // 8)
    )
    weight = jnp.where(mine, gated * (1.0 / 32768.0), 0.0)
    weight_hi = weight.astype(BF)
    comb_hi[...] = weight_hi
    comb_lo[...] = (weight - weight_hi.astype(F32)).astype(BF)

    go = go_v[...].astype(F32)
    blk = iota((128, 64), 1)
    own_blk = c * 4 + iota((128, 64), 0) // 32
    query_pos = jnp.sum(jnp.where(blk == own_blk, go, 0.0), axis=1, keepdims=True) * 32.0 + (
        iota((128, 1), 0) % 32
    ).astype(F32)
    wait(own_half, lc_r.at[0])
    wait(own_half, lc_r.at[1])
    q_copy.wait()
    eye = jnp.where(iota((128, 128), 0) == iota((128, 128), 1), 1.0, 0.0).astype(BF)
    queries = dot(eye, q[...], ((1,), (1,))).astype(BF)

    def score(i, top):
        keys = jnp.concatenate([lat[2 * i], lat[2 * i + 1]], axis=1)
        lane = iota((64, 256), 1)
        owner = jnp.where(iota((64, 256), 0) == i * 8 + lane // 32, 1.0, 0.0).astype(BF)
        base = dot(go.astype(BF), owner)
        key_pos = base * 32.0 + (iota((1, 256), 1) % 32).astype(F32)
        s = dot(queries, keys) * SCALE
        s = jnp.where(key_pos <= query_pos, s, -1e30)
        scores[i] = s
        return jnp.maximum(top, jnp.max(s, axis=1, keepdims=True))

    top = lax.fori_loop(0, 8, score, jnp.full((128, 1), -1e30, F32))

    def mix(i, carry):
        total, acc = carry
        p = jnp.exp(scores[i] - top)
        values = jnp.concatenate([lat[2 * i, :KV_RANK], lat[2 * i + 1, :KV_RANK]], axis=1)
        return total + jnp.sum(p, axis=1, keepdims=True), acc + dot(p.astype(BF), values, ((1,), (1,)))

    total, acc = lax.fori_loop(
        0, 8, mix, (jnp.zeros((128, 1), F32), jnp.zeros((128, KV_RANK), F32))
    )
    attn_ref[...] = (acc / total).astype(BF)

    wait(back.at[pl.ds(0, 63)], rt_r)
    rows = back[...].astype(F32).reshape(512, 128).astype(BF)
    mixed = dot(comb_hi[...], rows, ((0,), (0,))) + dot(comb_lo[...], rows, ((0,), (0,)))
    for j in range(4):
        width = min(128, 448 - 128 * j)
        moe_ref[:, 128 * j : 128 * j + width] = mixed[8 * j : 8 * j + 8, :width].astype(BF)

    wait(hall.at[0, 0, pl.ds(0, 3)], hx_s)
    wait(hall.at[0, pl.ds(0, 7)], hz_s)
    wait(hall.at[0], hc_s)
    for h in range(2):
        wait(part.at[h, pl.ds(0, 8)], rx_s.at[h])
        wait(part.at[h, pl.ds(0, 7)], ry_s.at[h])
        wait(inner.at[h, pl.ds(0, 7)], ay_s.at[h])
        wait(inner.at[h, pl.ds(0, 8)], ax_s.at[h])
    wait(ret.at[pl.ds(0, 63)], rt_s)
    wait(lat.at[pl.ds(0, 7), pl.ds(0, 288)], ly_s)
    wait(own_half, lx_s)
    wait(own_half, lc_s.at[0])
    wait(own_half, lc_s.at[1])


def per_device(queries, latents, group_order, hidden_b, expert_ids, gate_fixed, w_gate, w_up, w_down):
    hbm = pl.BlockSpec(memory_space=pltpu.HBM)
    vmem = pl.BlockSpec(memory_space=pltpu.VMEM)
    dma = pltpu.SemaphoreType.DMA
    return pl.pallas_call(
        kernel,
        out_shape=(
            pltpu.VMEM((128, 512), BF),
            pltpu.VMEM((8, 448), BF),
        ),
        in_specs=[hbm] * 9,
        out_specs=(vmem, vmem),
        scratch_shapes=[
            pltpu.VMEM((576, 128), BF),
            pltpu.VMEM((16, 576, 128), BF),
            pltpu.VMEM((512, 1024), BF),
            pltpu.VMEM((512, 1024), BF),
            pltpu.VMEM((448, 1024), BF),
            pltpu.VMEM((1, 64), I32),
            pltpu.VMEM((8, 448), BF),
            pltpu.VMEM((8, 8), I32),
            pltpu.VMEM((8, 8), I32),
            pltpu.VMEM((8, 512), F32),
            pltpu.VMEM((2, 8, 4, 16, 256), BF),
            pltpu.VMEM((2, 16, 16, 512), BF),
            pltpu.VMEM((2, 16, 16, 512), F32),
            pltpu.VMEM((2, 8, 16, 512), BF),
            pltpu.VMEM((2, 8, 16, 512), BF),
            pltpu.VMEM((2, 16, 16, 256), BF),
            pltpu.VMEM((128, 512), F32),
            pltpu.VMEM((64, 8, 128), BF),
            pltpu.VMEM((64, 8, 128), BF),
            pltpu.VMEM((512, 32), BF),
            pltpu.VMEM((512, 32), BF),
            pltpu.VMEM((8, 128, 256), F32),
            dma((3,)), dma, dma, dma((4,)),
            pltpu.SemaphoreType.REGULAR((3, 2)),
            pltpu.SemaphoreType.REGULAR((8,)),
            dma, dma((3,)), dma, dma((8,)), dma, dma,
            dma((2,)), dma((2, 8)), dma((2,)), dma((2,)),
            dma((2,)), dma((2,)), dma((2,)), dma((2,)),
            dma, dma,
            dma, dma, dma, dma, dma((2,)), dma((2,)),
        ],
        compiler_params=pltpu.CompilerParams(
            collective_id=0, has_side_effects=True, vmem_limit_bytes=60 << 20
        ),
        name="layer",
    )(
        queries.T, latents.T, group_order.reshape(1, 64), hidden_b, expert_ids, gate_fixed,
        w_gate, w_up, jnp.swapaxes(w_down, 1, 2),
    )


def solution(mesh):
    in_specs = (
        P("ctx", "exp"),
        P("ctx", None),
        P(),
        P("exp", "ctx"),
        P("exp", None),
        P("exp", None),
        P("exp", "ctx", None),
        P("exp", "ctx", None),
        P("exp", None, "ctx"),
    )
    out_specs = (P("ctx", "exp"), P("exp", "ctx"))
    return jax.shard_map(
        per_device, mesh=mesh, in_specs=in_specs, out_specs=out_specs, check_vma=False
    )
```
